512 devices in a mesh: lat: 32 (over y, z_lo, core), lon: 16 (over z_hi, x).
Axes of the slice: x: 4, y: 8, z: 8 (z_hi: 4, z_lo: 2; z = z_hi * 2 + z_lo), core: 2. Of those that a mesh axis runs over, the one named last changes fastest.
Arguments:
- adj_u: float32 [16, 2048, 2048], P(None, 'lat', 'lon'), may hold values from -6 to 6
- adj_v: float32 [16, 2048, 2048], P(None, 'lat', 'lon'), may hold values from -6 to 6
- adj_theta: float32 [16, 2048, 2048], P(None, 'lat', 'lon'), may hold values from -6 to 6
- adj_thick: float32 [16, 2048, 2048], P(None, 'lat', 'lon'), may hold values from -6 to 6
- theta_traj: float32 [16, 2048, 2048], P(None, 'lat', 'lon'), may hold values from 0.8 to 1.6
- dp_traj: float32 [16, 2048, 2048], P(None, 'lat', 'lon'), may hold values from 0.5 to 1.5
- cutoff: int32 [2048], replicated, may hold values from 32 to 511
- polar_flags: int32 [2048], replicated, may hold values from 0 to 1, as said below
Outputs:
- u_adjoint: float32 [16, 2048, 2048], P(None, 'lat', 'lon')
- v_adjoint: float32 [16, 2048, 2048], P(None, 'lat', 'lon')
- theta_adjoint: float32 [16, 2048, 2048], P(None, 'lat', 'lon')
- thickness_adjoint: float32 [16, 2048, 2048], P(None, 'lat', 'lon')
The draws below stay inside these ranges and needn't reach their ends.
Inputs may be any that keep to these rules, and one draw needn't show every extreme that they name: polar_flags is 1 on the first S rows and the last N rows and 0 between; S and N lie between 256 and 512, and one of them equals 512.
All inputs are finite; a program needn't handle non-finite values.
Results may differ from the reference program's by a relative error of at most 0.00011.
Values sent between devices are 32-bit elements; how exact they have to be, the bound alone decides.
No kernel may reach another device: no remote copies, remote signals or barrier semaphores. Data moves between devices by JAX's collectives and lax.ppermute only.
A program may use at most 64 MiB of HBM per device.

```python
import jax
import jax.numpy as jnp

NLON = 2048
LEV = 16
NLAT = 2048


def draw_polar_flags(key, part):
    key = jax.random.fold_in(key, 11)
    run_most = NLAT // 4
    run_least = NLAT // 8
    first_key, second_key = jax.random.split(key)
    other_run = jax.random.randint(first_key, (), run_least, run_most + 1)
    south_first = jax.random.randint(second_key, (), 0, 2)
    south_run = jnp.where(south_first == 1, run_most, other_run)
    north_run = jnp.where(south_first == 1, other_run, run_most)
    row_index = jnp.arange(NLAT, dtype=jnp.int32)
    polar_mask = (row_index < south_run) | (row_index >= NLAT - north_run)
    return polar_mask.astype(jnp.int32)


def with_ends(values, rng, low, largest):
    index_at = [jax.random.randint(jax.random.fold_in(rng, axis), (), 0, length) for axis, length in enumerate(values.shape)]
    main_axis = values.shape.index(max(values.shape))
    neighbour = index_at[:main_axis] + [(index_at[main_axis] + 1) % values.shape[main_axis]] + index_at[main_axis + 1:]
    return values.at[tuple(index_at)].set(low).at[tuple(neighbour)].set(largest)


def block_scale(rng, dims, pieces, least, high):
    factor_of, own = 1.0, jax.random.fold_in(rng, 6)
    for axis_at, shards_of in pieces:
        steps = jnp.exp(jax.random.uniform(jax.random.fold_in(own, axis_at), (shards_of,), jnp.float32, least / len(pieces), high / len(pieces)))
        factor_of = factor_of * jnp.repeat(steps, dims[axis_at] // shards_of).reshape([-1 if axis == axis_at else 1 for axis in range(len(dims))])
    return factor_of


def noise(key, dims, width, bound, cuts=(), kind=jnp.bfloat16):
    gain = block_scale(key, dims, cuts, -0.22, 0.18) if cuts else 1.0
    drawn = jax.random.normal(key, dims, jnp.float32) * width * gain
    return jnp.minimum(jnp.maximum(drawn, -bound), bound).astype(kind)


def setup_inputs(seed: int = 0) -> dict:
    seeds = jax.random.split(jax.random.key(seed), 9)
    adj_u = noise(seeds[0], (LEV, NLAT, NLON), 1.0, 6.0, ((1, 32), (2, 16)), jnp.float32)
    adj_v = noise(seeds[1], (LEV, NLAT, NLON), 1.0, 6.0, ((1, 32), (2, 16)), jnp.float32)
    adj_theta = noise(seeds[2], (LEV, NLAT, NLON), 1.0, 6.0, ((1, 32), (2, 16)), jnp.float32)
    adj_thick = noise(seeds[3], (LEV, NLAT, NLON), 1.0, 6.0, ((1, 32), (2, 16)), jnp.float32)
    theta_traj = jnp.clip(0.8 + 0.8 * jax.random.uniform(seeds[4], (LEV, NLAT, NLON), jnp.float32) ** block_scale(seeds[4], (LEV, NLAT, NLON), ((1, 32), (2, 16)), -0.2, 0.2), 0.8, 1.6)
    dp_traj = jnp.clip(0.5 + 1.0 * jax.random.uniform(seeds[5], (LEV, NLAT, NLON), jnp.float32) ** block_scale(seeds[5], (LEV, NLAT, NLON), ((1, 32), (2, 16)), -0.2, 0.2), 0.5, 1.5)
    cutoff = with_ends(jax.random.randint(seeds[6], (NLAT,), NLON // 64, NLON // 4), jax.random.fold_in(seeds[6], 1), NLON // 64, (NLON // 4) - 1).astype(jnp.int32)
    polar_flags = draw_polar_flags(jax.random.fold_in(seeds[8], 71), 0)
    return dict(adj_u=adj_u, adj_v=adj_v, adj_theta=adj_theta, adj_thick=adj_thick, theta_traj=theta_traj, dp_traj=dp_traj, cutoff=cutoff, polar_flags=polar_flags)


KAPPA = 0.3
CROSS = 0.2
MERID = 0.3

def row_geometry(row_index, total_rows):
    position = row_index.astype(jnp.float32)
    centre = jnp.pi * ((position + 0.5) / total_rows - 0.5)
    face = jnp.pi * ((position + 1.0) / total_rows - 0.5)
    return (jnp.cos(face), 1.0 / (jnp.cos(centre) + 0.25))

def north_of(field):
    return jnp.concatenate([field[:, 1:], jnp.zeros_like(field[:, :1])], axis=1)

def south_of(field):
    return jnp.concatenate([jnp.zeros_like(field[:, :1]), field[:, :-1]], axis=1)

def polar_filter(field, cutoff, polar_flags):
    length = field.shape[-1]
    wave = jnp.arange(length // 2 + 1, dtype=jnp.int32).astype(jnp.float32)
    limit = cutoff.astype(jnp.float32)[:, None]
    damping = jnp.where(wave[None] < limit, 1.0, (limit / jnp.maximum(wave[None], 1.0)) ** 2)
    damping = jnp.where(wave[None] < length // 2, damping, 0.0)
    spectrum = jnp.fft.rfft(field, axis=-1) * damping[None]
    smooth = jnp.fft.irfft(spectrum, n=length, axis=-1)
    return jnp.where(polar_flags[None, :, None] > 0, smooth, field)

def substep(wind_u, wind_v, theta_pert, thickness, theta_traj, dp_traj, cutoff, polar_flags):
    total_rows = wind_u.shape[1]
    face_cos, metric = row_geometry(jnp.arange(total_rows, dtype=jnp.int32), total_rows)
    face_cos = face_cos[None, :, None]
    metric = metric[None, :, None]
    depth_x = 0.5 * (dp_traj + jnp.roll(dp_traj, -1, axis=2))
    depth_y = 0.5 * (dp_traj + north_of(dp_traj))
    flux_x = depth_x * wind_u
    flux_y = depth_y * face_cos * wind_v
    change = -CROSS * metric * (flux_x - jnp.roll(flux_x, 1, axis=2)) - MERID * metric * (flux_y - south_of(flux_y))
    thick_new = thickness + change
    theta_new = theta_pert + KAPPA * theta_traj / dp_traj * change
    geopot = theta_traj * thick_new + dp_traj * theta_new
    u_mid = wind_u - CROSS * metric * (jnp.roll(geopot, -1, axis=2) - geopot)
    v_mid = wind_v - MERID * (north_of(geopot) - geopot)
    return (polar_filter(u_mid, cutoff, polar_flags), polar_filter(v_mid, cutoff, polar_flags), theta_new, thick_new)

def reference(adj_u, adj_v, adj_theta, adj_thick, theta_traj, dp_traj, cutoff, polar_flags):

    def forward(wind_u, wind_v, theta_pert, thickness):
        return substep(wind_u, wind_v, theta_pert, thickness, theta_traj, dp_traj, cutoff, polar_flags)
    zeros_field = jnp.zeros_like(adj_u)
    outputs, pullback = jax.vjp(forward, zeros_field, zeros_field, zeros_field, zeros_field)
    u_adjoint, v_adjoint, theta_adjoint, thickness_adjoint = pullback((adj_u, adj_v, adj_theta, adj_thick))
    return (u_adjoint, v_adjoint, theta_adjoint, thickness_adjoint)
```

```python
import functools

import jax
import jax.numpy as jnp
import numpy as np
from jax import lax
from jax.experimental import pallas as pl
from jax.experimental.pallas import tpu as pltpu
from jax.sharding import PartitionSpec as P

KAPPA = 0.3
CROSS = 0.2
MERID = 0.3
LANES = 128
PAD_ROWS = 8
VMEM_LIMIT = 24 * 1024 * 1024
VMEM_LARGE = 56 * 1024 * 1024


def filter_tables(segments, width):
    length = segments * width
    half = segments // 2
    b = np.arange(width)
    angle = 2.0 * np.pi * (np.outer(b, b) % width) / width
    cos, sin = np.cos(angle), np.sin(angle)
    forward = np.block([[cos, -sin], [sin, cos]])
    n = np.arange(2 * width)
    real_angle = 2.0 * np.pi * (np.outer(n, np.arange(width + 1)) % (2 * width)) / (2 * width)
    real_forward = np.concatenate([np.cos(real_angle), -np.sin(real_angle[:, 1:width])], axis=1)
    twist = 2.0 * np.pi * np.outer(np.arange(1, half), b) / length
    twist_tables = np.stack([np.cos(twist), np.sin(twist)])
    waves = np.zeros((half, 2 * width))
    waves[0] = half * np.concatenate([np.arange(width + 1), np.arange(1, width)])
    for c in range(1, half):
        waves[c] = np.tile(c + segments * b, 2)
    folded = np.minimum(waves, length - waves)
    scale = np.where(folded < length // 2, 2.0 / length, 0.0)
    scale[0, 0] = 1.0 / length
    bound = scale / np.maximum(folded, 1.0) ** 2

    def split(matrix):
        matrix = matrix.astype(np.float32)
        high = matrix.astype(jnp.bfloat16)
        low = (matrix - high.astype(np.float32)).astype(jnp.bfloat16)
        return [jnp.asarray(high), jnp.asarray(low)]

    matrices = split(forward) + split(real_forward) + split(forward.T) + split(real_forward.T)
    return (
        matrices,
        jnp.asarray(twist_tables, jnp.float32),
        jnp.asarray(np.stack([scale, bound]), jnp.float32),
    )


def split_product(values, high_ref, low_ref):
    high = values.astype(jnp.bfloat16)
    low = (values - high.astype(jnp.float32)).astype(jnp.bfloat16)
    product = functools.partial(jnp.dot, preferred_element_type=jnp.float32)
    return (
        product(high, high_ref[...])
        + (product(low, high_ref[...]) + product(high, low_ref[...]))
    )


A1, B1, G1 = (float(np.cos(np.pi / 8)), float(np.cos(np.pi / 4)), float(np.cos(3 * np.pi / 8)))
ODD = {
    1: ((A1, B1, G1), (G1, B1, A1), 1.0),
    3: ((G1, -B1, -A1), (A1, B1, -G1), -1.0),
    5: ((-G1, -B1, A1), (A1, -B1, -G1), 1.0),
    7: ((-A1, B1, -G1), (G1, -B1, A1), -1.0),
}


def segment_transform(x):
    e = [x[j] + x[j + 8] for j in range(8)]
    o = [x[j] - x[j + 8] for j in range(8)]
    f = [e[j] + e[j + 4] for j in range(4)]
    g = [e[j] - e[j + 4] for j in range(4)]
    out = {4: (f[0] - f[2], f[3] - f[1])}
    minus, plus = B1 * (g[1] - g[3]), B1 * (g[1] + g[3])
    out[2] = (g[0] + minus, -g[2] - plus)
    out[6] = (g[0] - minus, g[2] - plus)
    d = [o[j] - o[8 - j] for j in (1, 2, 3)]
    s = [o[j] + o[8 - j] for j in (1, 2, 3)]
    for c, (cos, sin, sign) in ODD.items():
        real = o[0] + cos[0] * d[0] + cos[1] * d[1] + cos[2] * d[2]
        imag = -(sign * o[4] + sin[0] * s[0] + sin[1] * s[1] + sin[2] * s[2])
        out[c] = (real, imag)
    return (f[0] + f[2], f[1] + f[3]), out


def segment_inverse(even, odd, z):
    quarter = [z[4][0], -z[4][1], -z[4][0], z[4][1]]
    f = [(even if j % 2 == 0 else odd) + quarter[j] for j in range(4)]
    r_minus, i_minus = z[2][0] - z[6][0], z[6][1] - z[2][1]
    r_plus, i_plus = z[2][0] + z[6][0], z[2][1] + z[6][1]
    g = [r_plus, B1 * (r_minus - i_plus), i_minus, -B1 * (r_minus + i_plus)]
    e = [f[j] + g[j] for j in range(4)] + [f[j] - g[j] for j in range(4)]
    o = [None] * 8
    o[0] = z[1][0] + z[3][0] + z[5][0] + z[7][0]
    o[4] = -(z[1][1] - z[3][1] + z[5][1] - z[7][1])
    for j in (1, 2, 3):
        d = sum(ODD[c][0][j - 1] * z[c][0] for c in (1, 3, 5, 7))
        s = -sum(ODD[c][1][j - 1] * z[c][1] for c in (1, 3, 5, 7))
        o[j] = d + s
        o[8 - j] = s - d
    return [e[j] + o[j] for j in range(8)] + [e[j] - o[j] for j in range(8)]


def ceil_to(value, step):
    return -(-value // step) * step


def filter_body(x_ref, limit_ref, flag_ref, twist_ref, weight_ref, matrices, out_ref, work_ref):
    segments, rows, width = x_ref.shape
    half = segments // 2
    base = ceil_to((half - 1) * rows, 16)
    forward, forward_low, real, real_low, back, back_low, real_back, real_back_low = matrices
    group = PAD_ROWS

    @pl.loop(0, rows // group)
    def _(step):
        at = pl.multiple_of(step * group, group)
        here = pl.ds(at, group)
        (even, odd), classes = segment_transform([x_ref[a, here, :] for a in range(segments)])
        to = pl.ds(pl.multiple_of(base + at, group), group)
        work_ref[to, :width] = even
        work_ref[to, width:] = odd
        for c in range(1, half):
            re, im = classes[c]
            cos, sin = twist_ref[0, c - 1 : c, :], twist_ref[1, c - 1 : c, :]
            to = pl.ds(pl.multiple_of((c - 1) * rows + at, group), group)
            work_ref[to, :width] = re * cos + im * sin
            work_ref[to, width:] = im * cos - re * sin

    limit = limit_ref[...]
    limit = limit * limit
    limit = jnp.concatenate([limit, limit], axis=1)

    def weights(c):
        return jnp.minimum(weight_ref[0, c : c + 1, :], limit * weight_ref[1, c : c + 1, :])

    spectrum = split_product(work_ref[:base, :], forward, forward_low)
    damping = [weights(c) for c in range(1, half)]
    if base > (half - 1) * rows:
        damping.append(jnp.zeros((base - (half - 1) * rows, 2 * width), jnp.float32))
    spectrum = spectrum * jnp.concatenate(damping, axis=0)
    work_ref[:base, :] = split_product(spectrum, back, back_low)
    spectrum = split_product(work_ref[base : base + rows, :], real, real_low) * weights(0)
    work_ref[base : base + rows, :] = split_product(spectrum, real_back, real_back_low)

    @pl.loop(0, rows // group)
    def _(step):
        at = pl.multiple_of(step * group, group)
        here = pl.ds(at, group)
        first = pl.ds(pl.multiple_of(base + at, group), group)
        z = {}
        for c in range(1, half):
            cos, sin = twist_ref[0, c - 1 : c, :], twist_ref[1, c - 1 : c, :]
            frm = pl.ds(pl.multiple_of((c - 1) * rows + at, group), group)
            re, im = work_ref[frm, :width], work_ref[frm, width:]
            z[c] = (re * cos - im * sin, re * sin + im * cos)
        smooth = segment_inverse(work_ref[first, :width], work_ref[first, width:], z)
        flagged = flag_ref[here, :] > 0.0
        for a in range(segments):
            out_ref[a, here, :] = jnp.where(flagged, smooth[a], x_ref[a, here, :])


def lane_index(shape):
    return lax.broadcasted_iota(jnp.int32, shape, len(shape) - 1)


def gather_columns(out_ref, start, rows, picks):
    shape = (rows, LANES)
    lanes = lane_index(shape)
    total = jnp.zeros(shape, jnp.float32)
    for q, a, lane in picks:
        column = jnp.broadcast_to(out_ref[a, start : start + rows, lane : lane + 1], shape)
        total = jnp.where(lanes == q, column, total)
    return total


def edge_kernel(u_first_ref, v_first_ref, v_last_ref, north_ref, south_ref):
    north_ref[0] = u_first_ref[:, 0, :]
    north_ref[1] = v_first_ref[:, 0, :]
    south_ref[...] = v_last_ref[:, PAD_ROWS - 1, :]


def pair_kernel(u_ref, v_ref, south_ref, north_ref, out_ref):
    levels, rows, width = u_ref.shape
    main = 2 * rows
    out_ref[:, :rows, :] = u_ref[...]
    out_ref[:, rows:main, :] = v_ref[...]
    out_ref[:, main:, :] = jnp.zeros((levels, PAD_ROWS, width), jnp.float32)
    out_ref[:, main, :] = south_ref[...]
    out_ref[:, main + 1, :] = north_ref[1]
    out_ref[:, main + 2, :] = north_ref[0]


def rows_kernel(limits_ref, flags_ref, limit_block_ref, flag_block_ref, limit_out, flag_out):
    rows = (limit_out.shape[0] - PAD_ROWS) // 2
    count = limits_ref.shape[0]
    first = lax.axis_index("lat") * rows
    block, part = first // LANES, (first % LANES) // rows
    south, north = jnp.maximum(first - 1, 0), jnp.minimum(first + rows, count - 1)
    sub = lax.broadcasted_iota(jnp.int32, (PAD_ROWS, LANES), 0)
    for line_ref, scalar_ref, out_ref in (
        (limit_block_ref, limits_ref, limit_out),
        (flag_block_ref, flags_ref, flag_out),
    ):
        line = jnp.broadcast_to(line_ref[pl.ds(block, 1), :].astype(jnp.float32), (LANES, LANES)).T
        own = line[:rows]
        for p in range(1, LANES // rows):
            own = jnp.where(part == p, line[p * rows : (p + 1) * rows], own)
        out_ref[:rows, :] = own
        out_ref[rows : 2 * rows, :] = own
        tail = jnp.where(sub == 0, scalar_ref[south], scalar_ref[north])
        out_ref[2 * rows :, :] = tail.astype(jnp.float32)


def filter_kernel(x_ref, limit_ref, flag_ref, geo_ref, twist_ref, weight_ref, *rest):
    matrices, (out_ref, work_ref) = rest[:8], rest[8:]
    segments, tall, width = x_ref.shape
    main = tall - PAD_ROWS
    rows = main // 2
    metric = geo_ref[0, :rows, :]
    metric_north = geo_ref[0, rows : rows + 1, :]
    edge = lane_index((1, width)) == 0
    filter_body(x_ref, limit_ref, flag_ref, twist_ref, weight_ref, matrices, out_ref, work_ref)
    u_north = [out_ref[a, main + 2 : main + 3, :] for a in range(segments)]
    rolled = [pltpu.roll(u_north[a], 1, 1) for a in range(segments)]
    last = width - 1
    ahead = [(a, (a + 1) % segments, 0) for a in range(segments)]
    behind = [(segments + a, (a - 1) % segments, last) for a in range(segments)]
    own = [(a, a, last) for a in range(segments)]
    side = gather_columns(out_ref, 0, rows, ahead + behind) - gather_columns(out_ref, 0, rows, own)
    v_ahead = gather_columns(out_ref, rows, rows + 1, ahead)
    v_body = v_ahead[:rows]
    top = lax.broadcasted_iota(jnp.int32, (rows, LANES), 0) == 0
    v_south = jnp.where(top, v_ahead[rows : rows + 1], pltpu.roll(v_body, 1, 0))
    mixed = CROSS * metric * side + MERID * (v_body - v_south)
    columns = jnp.where(lane_index((rows, LANES)) < segments, mixed, side)
    columns = jnp.concatenate([columns, jnp.zeros((LANES - rows, LANES), jnp.float32)], axis=0).T
    for a in range(segments):
        west = jnp.where(edge, rolled[a - 1], rolled[a])
        north = CROSS * metric_north * (u_north[a] - west) + MERID * (
            out_ref[a, main + 1 : main + 2, :] - out_ref[a, main - 1 : main, :]
        )
        out_ref[a, main + 1 : main + 2, :] = north
        out_ref[a, main + 2 : main + 3, :] = columns[a : a + 1]
        out_ref[a, main + 3 : main + 4, :] = columns[segments + a : segments + a + 1]


def substep_kernel(
    winds_ref, thick_ref, theta_ref, traj_ref, depth_ref, geo_ref, north_ref, east_ref,
    u_out, v_out, theta_out, thick_out,
):
    levels, rows, width = thick_ref.shape
    main = 2 * rows
    metric, face = geo_ref[0, :rows, :], geo_ref[1, :rows, :]
    metric_north = geo_ref[0, rows : rows + 1, :]
    shape = (rows, width)
    lanes, sub = lane_index(shape), lax.broadcasted_iota(jnp.int32, shape, 0)
    first_lane, last_lane = lanes == 0, lanes == width - 1
    first_row, last_row = sub == 0, sub == rows - 1
    lines = []
    for k in range(levels):
        ga_east = winds_ref[k, main + 2 : main + 3, :]
        lines.append(east_ref[0, k : k + 1, :] + (1.0 + KAPPA) * east_ref[1, k : k + 1, :] * ga_east)
    for k in range(levels):
        lines.append(east_ref[2, k : k + 1, :])
    for k in range(levels):
        lines.append(winds_ref[k, main + 3 : main + 4, :])
    lines.append(jnp.zeros((LANES - 3 * levels, width), jnp.float32))
    columns = jnp.concatenate(lines, axis=0).T
    for k in range(levels):
        ua, va = winds_ref[k, :rows, :], winds_ref[k, rows:main, :]
        traj, depth = traj_ref[k], depth_ref[k]
        e_east = jnp.broadcast_to(columns[:rows, k : k + 1], shape)
        depth_east = jnp.broadcast_to(columns[:rows, levels + k : levels + k + 1], shape)
        u_west = jnp.broadcast_to(columns[:rows, 2 * levels + k : 2 * levels + k + 1], shape)
        west = jnp.where(first_lane, u_west, pltpu.roll(ua, 1, 1))
        south = jnp.where(first_row, winds_ref[k, main : main + 1, :], pltpu.roll(va, 1, 0))
        ga = CROSS * metric * (ua - west) + MERID * (va - south)
        thick = thick_ref[k] + traj * ga
        theta = theta_ref[k] + depth * ga
        e = thick + KAPPA * (traj / depth) * theta
        e_shift = jnp.where(last_lane, e_east, pltpu.roll(e, width - 1, 1))
        depth_shift = jnp.where(last_lane, depth_east, pltpu.roll(depth, width - 1, 1))
        u_out[k] = ua + (0.5 * CROSS) * (depth + depth_shift) * metric * (e_shift - e)
        e_north = north_ref[0, k : k + 1, :] + (1.0 + KAPPA) * north_ref[1, k : k + 1, :] * winds_ref[k, main + 1 : main + 2, :]
        me = metric * e
        me_shift = jnp.where(last_row, metric_north * e_north, pltpu.roll(me, rows - 1, 0))
        depth_up = jnp.where(last_row, north_ref[2, k : k + 1, :], pltpu.roll(depth, rows - 1, 0))
        v_out[k] = va + (0.5 * MERID) * (depth + depth_up) * face * (me_shift - me)
        theta_out[k] = theta
        thick_out[k] = thick


def row_geometry(row_index, total_rows):
    position = row_index.astype(jnp.float32)
    centre = jnp.pi * ((position + 0.5) / total_rows - 0.5)
    face = jnp.pi * ((position + 1.0) / total_rows - 0.5)
    return (jnp.cos(face), 1.0 / (jnp.cos(centre) + 0.25))


def spread(column):
    return jnp.broadcast_to(column[:, None], (column.shape[0], LANES))


def swap(blocks):
    return lax.all_to_all(blocks, "lon", split_axis=0, concat_axis=0, tiled=True)


def shards(adj_u, adj_v, adj_theta, adj_thick, theta_traj, dp_traj, cutoff, polar_flags):
    levels, rows, width = adj_u.shape
    bands, segments = lax.axis_size("lat"), lax.axis_size("lon")
    band = lax.axis_index("lat")
    total_rows = rows * bands
    tall = 2 * rows + PAD_ROWS
    matrices, twist, weight = filter_tables(segments, width)
    params = pltpu.CompilerParams(vmem_limit_bytes=VMEM_LIMIT)
    large = pltpu.CompilerParams(vmem_limit_bytes=VMEM_LARGE)
    in_vmem = pl.BlockSpec(memory_space=pltpu.VMEM)

    north_to_south = [(i + 1, i) for i in range(bands - 1)]
    south_to_north = [(i, i + 1) for i in range(bands - 1)]
    east_to_west = [((i + 1) % segments, i) for i in range(segments)]

    block = lambda at: pl.BlockSpec((levels, PAD_ROWS, width), lambda i, at=at: (0, at, 0))
    first, last = block(0), block(rows // PAD_ROWS - 1)
    to_south, to_north = pl.pallas_call(
        edge_kernel,
        grid=(1,),
        in_specs=[first, first, last],
        out_specs=[
            pl.BlockSpec((2, levels, width), lambda i: (0, 0, 0)),
            pl.BlockSpec((levels, width), lambda i: (0, 0)),
        ],
        out_shape=[
            jax.ShapeDtypeStruct((2, levels, width), jnp.float32),
            jax.ShapeDtypeStruct((levels, width), jnp.float32),
        ],
        compiler_params=large,
    )(adj_u, adj_v, adj_v)
    from_north = lax.ppermute(to_south, "lat", north_to_south)
    from_south = lax.ppermute(to_north, "lat", south_to_north)
    step = 8
    field = pl.BlockSpec((step, rows, width), lambda i: (i, 0, 0))
    pair = pl.pallas_call(
        pair_kernel,
        grid=(levels // step,),
        in_specs=[
            field,
            field,
            pl.BlockSpec((step, width), lambda i: (i, 0)),
            pl.BlockSpec((2, step, width), lambda i: (0, i, 0)),
        ],
        out_specs=pl.BlockSpec((step, tall, width), lambda i: (i, 0, 0)),
        out_shape=jax.ShapeDtypeStruct((levels, tall, width), jnp.float32),
        compiler_params=large,
    )(adj_u, adj_v, from_south, from_north)
    circles = swap(pair)

    def edge_sum(pick):
        theta, depth = pick(theta_traj), pick(dp_traj)
        return pick(adj_thick) + KAPPA * (theta / depth) * pick(adj_theta), theta, depth

    north = jnp.stack(edge_sum(lambda x: x[:, 0, :]))
    north = lax.ppermute(north, "lat", north_to_south)
    east = jnp.stack(edge_sum(lambda x: x[:, :, 0]))
    east = jnp.pad(east, ((0, 0), (0, 0), (0, LANES - rows)))
    east = lax.ppermute(east, "lon", east_to_west)

    whole = pl.BlockSpec(memory_space=pltpu.SMEM)
    spread_rows = jax.ShapeDtypeStruct((tall, LANES), jnp.float32)
    limit, flag = pl.pallas_call(
        rows_kernel,
        in_specs=[whole, whole, in_vmem, in_vmem],
        out_specs=[in_vmem, in_vmem],
        out_shape=[spread_rows, spread_rows],
        compiler_params=params,
    )(cutoff, polar_flags, cutoff.reshape(-1, LANES), polar_flags.reshape(-1, LANES))
    face, metric = row_geometry(band * rows + jnp.arange(rows + PAD_ROWS, dtype=jnp.int32), total_rows)
    geo = jnp.stack([spread(metric), spread(face)])

    half = segments // 2
    depth_of_work = ceil_to((half - 1) * tall, 16) + ceil_to(tall, 16)
    smooth = pl.pallas_call(
        filter_kernel,
        out_shape=jax.ShapeDtypeStruct((segments, tall, width), jnp.float32),
        scratch_shapes=[
            pltpu.VMEM((depth_of_work, 2 * width), jnp.float32),
        ],
        compiler_params=params,
    )(circles, limit, flag, geo, twist, weight, *matrices)
    winds = swap(smooth)

    step = 4
    field = pl.BlockSpec((step, rows, width), lambda i: (i, 0, 0))
    lines = pl.BlockSpec((3, None, step, width), lambda i: (0, i, 0, 0))
    grouped = lambda x: x[:3].reshape(3, levels // step, step, width)
    return pl.pallas_call(
        substep_kernel,
        grid=(levels // step,),
        in_specs=[
            pl.BlockSpec((step, tall, width), lambda i: (i, 0, 0)),
            field,
            field,
            field,
            field,
            pl.BlockSpec((2, rows + PAD_ROWS, width), lambda i: (0, 0, 0)),
            lines,
            lines,
        ],
        out_specs=[field] * 4,
        out_shape=[jax.ShapeDtypeStruct(adj_u.shape, jnp.float32)] * 4,
        compiler_params=params,
    )(winds, adj_thick, adj_theta, theta_traj, dp_traj, geo, grouped(north), grouped(east))


def solution(mesh):
    field = P(None, "lat", "lon")
    return jax.shard_map(
        shards,
        mesh=mesh,
        in_specs=(field,) * 6 + (P(), P()),
        out_specs=(field,) * 4,
        check_vma=False,
    )
```

```python
import functools

import jax
import jax.numpy as jnp
import numpy as np
from jax import lax
from jax.experimental import pallas as pl
from jax.experimental.pallas import tpu as pltpu
from jax.sharding import PartitionSpec as P

KAPPA = 0.3
CROSS = 0.2
MERID = 0.3
LANES = 128
PAD_ROWS = 8
VMEM_LIMIT = 24 * 1024 * 1024
VMEM_LARGE = 56 * 1024 * 1024


def filter_tables(segments, width):
    length = segments * width
    half = segments // 2
    b = np.arange(width)
    angle = 2.0 * np.pi * (np.outer(b, b) % width) / width
    cos, sin = np.cos(angle), np.sin(angle)
    forward = np.block([[cos, -sin], [sin, cos]])
    n = np.arange(2 * width)
    real_angle = 2.0 * np.pi * (np.outer(n, np.arange(width + 1)) % (2 * width)) / (2 * width)
    real_forward = np.concatenate([np.cos(real_angle), -np.sin(real_angle[:, 1:width])], axis=1)
    twist = 2.0 * np.pi * np.outer(np.arange(1, half), b) / length
    twist_tables = np.stack([np.cos(twist), np.sin(twist)])
    waves = np.zeros((half, 2 * width))
    waves[0] = half * np.concatenate([np.arange(width + 1), np.arange(1, width)])
    for c in range(1, half):
        waves[c] = np.tile(c + segments * b, 2)
    folded = np.minimum(waves, length - waves)
    scale = np.where(folded < length // 2, 2.0 / length, 0.0)
    scale[0, 0] = 1.0 / length
    bound = scale / np.maximum(folded, 1.0) ** 2

    def split(matrix):
        matrix = matrix.astype(np.float32)
        high = matrix.astype(jnp.bfloat16)
        low = (matrix - high.astype(np.float32)).astype(jnp.bfloat16)
        return [jnp.asarray(high), jnp.asarray(low)]

    matrices = split(forward) + split(real_forward) + split(forward.T) + split(real_forward.T)
    return (
        matrices,
        jnp.asarray(twist_tables, jnp.float32),
        jnp.asarray(np.stack([scale, bound]), jnp.float32),
    )


def split_product(values, high_ref, low_ref):
    high = values.astype(jnp.bfloat16)
    low = (values - high.astype(jnp.float32)).astype(jnp.bfloat16)
    product = functools.partial(jnp.dot, preferred_element_type=jnp.float32)
    return (
        product(high, high_ref[...])
        + (product(low, high_ref[...]) + product(high, low_ref[...]))
    )


A1, B1, G1 = (float(np.cos(np.pi / 8)), float(np.cos(np.pi / 4)), float(np.cos(3 * np.pi / 8)))
ODD = {
    1: ((A1, B1, G1), (G1, B1, A1), 1.0),
    3: ((G1, -B1, -A1), (A1, B1, -G1), -1.0),
    5: ((-G1, -B1, A1), (A1, -B1, -G1), 1.0),
    7: ((-A1, B1, -G1), (G1, -B1, A1), -1.0),
}


def segment_transform(x):
    e = [x[j] + x[j + 8] for j in range(8)]
    o = [x[j] - x[j + 8] for j in range(8)]
    f = [e[j] + e[j + 4] for j in range(4)]
    g = [e[j] - e[j + 4] for j in range(4)]
    out = {4: (f[0] - f[2], f[3] - f[1])}
    minus, plus = B1 * (g[1] - g[3]), B1 * (g[1] + g[3])
    out[2] = (g[0] + minus, -g[2] - plus)
    out[6] = (g[0] - minus, g[2] - plus)
    d = [o[j] - o[8 - j] for j in (1, 2, 3)]
    s = [o[j] + o[8 - j] for j in (1, 2, 3)]
    for c, (cos, sin, sign) in ODD.items():
        real = o[0] + cos[0] * d[0] + cos[1] * d[1] + cos[2] * d[2]
        imag = -(sign * o[4] + sin[0] * s[0] + sin[1] * s[1] + sin[2] * s[2])
        out[c] = (real, imag)
    return (f[0] + f[2], f[1] + f[3]), out


def segment_inverse(even, odd, z):
    quarter = [z[4][0], -z[4][1], -z[4][0], z[4][1]]
    f = [(even if j % 2 == 0 else odd) + quarter[j] for j in range(4)]
    r_minus, i_minus = z[2][0] - z[6][0], z[6][1] - z[2][1]
    r_plus, i_plus = z[2][0] + z[6][0], z[2][1] + z[6][1]
    g = [r_plus, B1 * (r_minus - i_plus), i_minus, -B1 * (r_minus + i_plus)]
    e = [f[j] + g[j] for j in range(4)] + [f[j] - g[j] for j in range(4)]
    o = [None] * 8
    o[0] = z[1][0] + z[3][0] + z[5][0] + z[7][0]
    o[4] = -(z[1][1] - z[3][1] + z[5][1] - z[7][1])
    for j in (1, 2, 3):
        d = sum(ODD[c][0][j - 1] * z[c][0] for c in (1, 3, 5, 7))
        s = -sum(ODD[c][1][j - 1] * z[c][1] for c in (1, 3, 5, 7))
        o[j] = d + s
        o[8 - j] = s - d
    return [e[j] + o[j] for j in range(8)] + [e[j] - o[j] for j in range(8)]


def ceil_to(value, step):
    return -(-value // step) * step


def filter_body(x_ref, limit_ref, flag_ref, twist_ref, weight_ref, matrices, out_ref, work_ref):
    segments, rows, width = x_ref.shape
    half = segments // 2
    base = ceil_to((half - 1) * rows, 16)
    forward, forward_low, real, real_low, back, back_low, real_back, real_back_low = matrices
    group = PAD_ROWS

    @pl.loop(0, rows // group)
    def _(step):
        at = pl.multiple_of(step * group, group)
        here = pl.ds(at, group)
        (even, odd), classes = segment_transform([x_ref[a, here, :] for a in range(segments)])
        to = pl.ds(pl.multiple_of(base + at, group), group)
        work_ref[to, :width] = even
        work_ref[to, width:] = odd
        for c in range(1, half):
            re, im = classes[c]
            cos, sin = twist_ref[0, c - 1 : c, :], twist_ref[1, c - 1 : c, :]
            to = pl.ds(pl.multiple_of((c - 1) * rows + at, group), group)
            work_ref[to, :width] = re * cos + im * sin
            work_ref[to, width:] = im * cos - re * sin

    limit = limit_ref[:rows, :]
    limit = limit * limit
    limit = jnp.concatenate([limit, limit], axis=1)

    def weights(c):
        return jnp.minimum(weight_ref[0, c : c + 1, :], limit * weight_ref[1, c : c + 1, :])

    spectrum = split_product(work_ref[:base, :], forward, forward_low)
    damping = [weights(c) for c in range(1, half)]
    if base > (half - 1) * rows:
        damping.append(jnp.zeros((base - (half - 1) * rows, 2 * width), jnp.float32))
    spectrum = spectrum * jnp.concatenate(damping, axis=0)
    work_ref[:base, :] = split_product(spectrum, back, back_low)
    spectrum = split_product(work_ref[base : base + rows, :], real, real_low) * weights(0)
    work_ref[base : base + rows, :] = split_product(spectrum, real_back, real_back_low)

    @pl.loop(0, rows // group)
    def _(step):
        at = pl.multiple_of(step * group, group)
        here = pl.ds(at, group)
        first = pl.ds(pl.multiple_of(base + at, group), group)
        z = {}
        for c in range(1, half):
            cos, sin = twist_ref[0, c - 1 : c, :], twist_ref[1, c - 1 : c, :]
            frm = pl.ds(pl.multiple_of((c - 1) * rows + at, group), group)
            re, im = work_ref[frm, :width], work_ref[frm, width:]
            z[c] = (re * cos - im * sin, re * sin + im * cos)
        smooth = segment_inverse(work_ref[first, :width], work_ref[first, width:], z)
        flagged = flag_ref[here, :] > 0.0
        for a in range(segments):
            out_ref[a, here, :] = jnp.where(flagged, smooth[a], x_ref[a, here, :])


def lane_index(shape):
    return lax.broadcasted_iota(jnp.int32, shape, len(shape) - 1)


def gather_columns(out_ref, rows, picks):
    shape = (rows, LANES)
    lanes = lane_index(shape)
    total = jnp.zeros(shape, jnp.float32)
    for q, a, lane in picks:
        column = jnp.broadcast_to(out_ref[a, :rows, lane : lane + 1], shape)
        total = jnp.where(lanes == q, column, total)
    return total


def edge_kernel(u_ref, v_first_ref, v_last_ref, thick_ref, theta_ref, traj_ref, depth_ref, north_ref, south_ref):
    traj, depth = traj_ref[:, 0, :], depth_ref[:, 0, :]
    north_ref[0] = thick_ref[:, 0, :] + KAPPA * (traj / depth) * theta_ref[:, 0, :]
    north_ref[1] = traj
    north_ref[2] = depth
    north_ref[3] = u_ref[:, 0, :]
    north_ref[4] = v_first_ref[:, 0, :]
    south_ref[...] = v_last_ref[:, PAD_ROWS - 1, :]


def pair_kernel(v_ref, south_ref, north_ref, out_ref):
    rows = v_ref.shape[1]
    out_ref[:, :rows, :] = v_ref[...]
    out_ref[:, rows:, :] = jnp.zeros(out_ref[:, rows:, :].shape, jnp.float32)
    out_ref[:, rows, :] = south_ref[...]
    out_ref[:, rows + 1, :] = north_ref[4]
    out_ref[:, rows + 2, :] = north_ref[3]


def rows_kernel(limits_ref, flags_ref, limit_block_ref, flag_block_ref, limit_out, flag_out, line_ref):
    rows = limit_out.shape[0] - PAD_ROWS
    count = limits_ref.shape[0]
    first = lax.axis_index("lat") * rows
    south, north = jnp.maximum(first - 1, 0), jnp.minimum(first + rows, count - 1)
    sub = lax.broadcasted_iota(jnp.int32, (PAD_ROWS, LANES), 0)
    for block_ref, scalar_ref, out_ref in (
        (limit_block_ref, limits_ref, limit_out),
        (flag_block_ref, flags_ref, flag_out),
    ):
        line = block_ref[pl.ds(first // LANES, 1), :].astype(jnp.float32)
        line_ref[...] = jnp.broadcast_to(line, (LANES, LANES)).T
        out_ref[:rows, :] = line_ref[pl.ds(pl.multiple_of(first % LANES, rows), rows), :]
        tail = jnp.where(sub == 0, scalar_ref[south], scalar_ref[north])
        out_ref[rows:, :] = tail.astype(jnp.float32)


def filter_u_kernel(x_ref, limit_ref, flag_ref, twist_ref, weight_ref, *rest):
    matrices, (out_ref, side_ref, smooth_ref, work_ref, sem) = rest[:8], rest[8:]
    segments, rows, width = x_ref.shape
    filter_body(x_ref, limit_ref, flag_ref, twist_ref, weight_ref, matrices, smooth_ref, work_ref)
    copy = pltpu.make_async_copy(smooth_ref, out_ref.at[:, :rows, :], sem)
    copy.start()
    last = width - 1
    ahead = [(a, (a + 1) % segments, 0) for a in range(segments)]
    behind = [(segments + a, (a - 1) % segments, last) for a in range(segments)]
    own = [(a, a, last) for a in range(segments)]
    side_ref[...] = gather_columns(smooth_ref, rows, ahead + behind) - gather_columns(smooth_ref, rows, own)
    copy.wait()


def filter_v_kernel(x_ref, limit_ref, flag_ref, geo_ref, side_ref, twist_ref, weight_ref, *rest):
    matrices, (_, out_ref, smooth_ref, work_ref, sem) = rest[:8], rest[8:]
    segments, tall, width = x_ref.shape
    rows = tall - PAD_ROWS
    filter_body(x_ref, limit_ref, flag_ref, twist_ref, weight_ref, matrices, smooth_ref, work_ref)
    metric = geo_ref[0, :rows, :]
    metric_north = geo_ref[0, rows : rows + 1, :]
    edge = lane_index((1, width)) == 0
    u_north = [smooth_ref[a, rows + 2 : rows + 3, :] for a in range(segments)]
    rolled = [pltpu.roll(u_north[a], 1, 1) for a in range(segments)]
    ahead = [(a, (a + 1) % segments, 0) for a in range(segments)]
    v_ahead = gather_columns(smooth_ref, rows + 1, ahead)
    v_body = v_ahead[:rows]
    top = lax.broadcasted_iota(jnp.int32, (rows, LANES), 0) == 0
    v_south = jnp.where(top, v_ahead[rows : rows + 1], pltpu.roll(v_body, 1, 0))
    side = side_ref[...]
    mixed = CROSS * metric * side + MERID * (v_body - v_south)
    columns = jnp.where(lane_index((rows, LANES)) < segments, mixed, side)
    columns = jnp.concatenate([columns, jnp.zeros((LANES - rows, LANES), jnp.float32)], axis=0).T
    for a in range(segments):
        west = jnp.where(edge, rolled[a - 1], rolled[a])
        smooth_ref[a, rows + 1 : rows + 2, :] = CROSS * metric_north * (u_north[a] - west) + MERID * (
            smooth_ref[a, rows + 1 : rows + 2, :] - smooth_ref[a, rows - 1 : rows, :]
        )
        smooth_ref[a, rows + 2 : rows + 3, :] = columns[a : a + 1]
        smooth_ref[a, rows + 3 : rows + 4, :] = columns[segments + a : segments + a + 1]
    copy = pltpu.make_async_copy(smooth_ref, out_ref.at[:, rows:, :], sem)
    copy.start()
    copy.wait()


def substep_kernel(
    winds_ref, thick_ref, theta_ref, traj_ref, depth_ref, geo_ref, north_ref, east_ref,
    u_out, v_out, theta_out, thick_out,
):
    levels, rows, width = thick_ref.shape
    main = 2 * rows
    metric, face = geo_ref[0, :rows, :], geo_ref[1, :rows, :]
    metric_north = geo_ref[0, rows : rows + 1, :]
    shape = (rows, width)
    lanes, sub = lane_index(shape), lax.broadcasted_iota(jnp.int32, shape, 0)
    first_lane, last_lane = lanes == 0, lanes == width - 1
    first_row, last_row = sub == 0, sub == rows - 1
    lines = []
    for k in range(levels):
        ga_east = winds_ref[k, main + 2 : main + 3, :]
        lines.append(east_ref[0, k : k + 1, :] + (1.0 + KAPPA) * east_ref[1, k : k + 1, :] * ga_east)
    for k in range(levels):
        lines.append(east_ref[2, k : k + 1, :])
    for k in range(levels):
        lines.append(winds_ref[k, main + 3 : main + 4, :])
    lines.append(jnp.zeros((LANES - 3 * levels, width), jnp.float32))
    columns = jnp.concatenate(lines, axis=0).T
    for k in range(levels):
        ua, va = winds_ref[k, :rows, :], winds_ref[k, rows:main, :]
        traj, depth = traj_ref[k], depth_ref[k]
        e_east = jnp.broadcast_to(columns[:rows, k : k + 1], shape)
        depth_east = jnp.broadcast_to(columns[:rows, levels + k : levels + k + 1], shape)
        u_west = jnp.broadcast_to(columns[:rows, 2 * levels + k : 2 * levels + k + 1], shape)
        west = jnp.where(first_lane, u_west, pltpu.roll(ua, 1, 1))
        south = jnp.where(first_row, winds_ref[k, main : main + 1, :], pltpu.roll(va, 1, 0))
        ga = CROSS * metric * (ua - west) + MERID * (va - south)
        thick = thick_ref[k] + traj * ga
        theta = theta_ref[k] + depth * ga
        e = thick + KAPPA * (traj / depth) * theta
        e_shift = jnp.where(last_lane, e_east, pltpu.roll(e, width - 1, 1))
        depth_shift = jnp.where(last_lane, depth_east, pltpu.roll(depth, width - 1, 1))
        u_out[k] = ua + (0.5 * CROSS) * (depth + depth_shift) * metric * (e_shift - e)
        e_north = north_ref[0, k : k + 1, :] + (1.0 + KAPPA) * north_ref[1, k : k + 1, :] * winds_ref[k, main + 1 : main + 2, :]
        me = metric * e
        me_shift = jnp.where(last_row, metric_north * e_north, pltpu.roll(me, rows - 1, 0))
        depth_up = jnp.where(last_row, north_ref[2, k : k + 1, :], pltpu.roll(depth, rows - 1, 0))
        v_out[k] = va + (0.5 * MERID) * (depth + depth_up) * face * (me_shift - me)
        theta_out[k] = theta
        thick_out[k] = thick


def row_geometry(row_index, total_rows):
    position = row_index.astype(jnp.float32)
    centre = jnp.pi * ((position + 0.5) / total_rows - 0.5)
    face = jnp.pi * ((position + 1.0) / total_rows - 0.5)
    return (jnp.cos(face), 1.0 / (jnp.cos(centre) + 0.25))


def spread(column):
    return jnp.broadcast_to(column[:, None], (column.shape[0], LANES))


def swap(blocks):
    return lax.all_to_all(blocks, "lon", split_axis=0, concat_axis=0, tiled=True)


def shards(adj_u, adj_v, adj_theta, adj_thick, theta_traj, dp_traj, cutoff, polar_flags):
    levels, rows, width = adj_u.shape
    bands, segments = lax.axis_size("lat"), lax.axis_size("lon")
    band = lax.axis_index("lat")
    total_rows = rows * bands
    tall, whole_block = rows + PAD_ROWS, 2 * rows + PAD_ROWS
    matrices, twist, weight = filter_tables(segments, width)
    params = pltpu.CompilerParams(vmem_limit_bytes=VMEM_LIMIT)
    large = pltpu.CompilerParams(vmem_limit_bytes=VMEM_LARGE)
    in_vmem = pl.BlockSpec(memory_space=pltpu.VMEM)
    in_hbm = pl.BlockSpec(memory_space=pltpu.HBM)
    in_smem = pl.BlockSpec(memory_space=pltpu.SMEM)
    f32 = lambda *shape: jax.ShapeDtypeStruct(shape, jnp.float32)
    north_to_south = [(i + 1, i) for i in range(bands - 1)]
    south_to_north = [(i, i + 1) for i in range(bands - 1)]
    east_to_west = [((i + 1) % segments, i) for i in range(segments)]

    circles_u = swap(adj_u)

    block = lambda at: pl.BlockSpec((levels, PAD_ROWS, width), lambda i, at=at: (0, at, 0))
    first, last = block(0), block(rows // PAD_ROWS - 1)
    to_south, to_north = pl.pallas_call(
        edge_kernel,
        grid=(1,),
        in_specs=[first, first, last, first, first, first, first],
        out_specs=[
            pl.BlockSpec((5, levels, width), lambda i: (0, 0, 0)),
            pl.BlockSpec((levels, width), lambda i: (0, 0)),
        ],
        out_shape=[f32(5, levels, width), f32(levels, width)],
        compiler_params=large,
    )(adj_u, adj_v, adj_v, adj_thick, adj_theta, theta_traj, dp_traj)
    north = lax.ppermute(to_south, "lat", north_to_south)
    south = lax.ppermute(to_north, "lat", south_to_north)
    step = 8
    circles_v = swap(
        pl.pallas_call(
            pair_kernel,
            grid=(levels // step,),
            in_specs=[
                pl.BlockSpec((step, rows, width), lambda i: (i, 0, 0)),
                pl.BlockSpec((step, width), lambda i: (i, 0)),
                pl.BlockSpec((5, step, width), lambda i: (0, i, 0)),
            ],
            out_specs=pl.BlockSpec((step, tall, width), lambda i: (i, 0, 0)),
            out_shape=f32(levels, tall, width),
            compiler_params=large,
        )(adj_v, south, north)
    )

    first_column = lambda x: x[:, :, 0]
    traj, depth = first_column(theta_traj), first_column(dp_traj)
    change = first_column(adj_thick) + KAPPA * (traj / depth) * first_column(adj_theta)
    east = jnp.stack([change, traj, depth])
    east = jnp.pad(east, ((0, 0), (0, 0), (0, LANES - rows)))
    east = lax.ppermute(east, "lon", east_to_west)

    limit, flag = pl.pallas_call(
        rows_kernel,
        in_specs=[in_smem, in_smem, in_vmem, in_vmem],
        out_specs=[in_vmem] * 2,
        out_shape=[f32(tall, LANES)] * 2,
        scratch_shapes=[pltpu.VMEM((LANES, LANES), jnp.float32)],
        compiler_params=params,
    )(cutoff, polar_flags, cutoff.reshape(-1, LANES), polar_flags.reshape(-1, LANES))
    face, metric = row_geometry(band * rows + jnp.arange(tall, dtype=jnp.int32), total_rows)
    geo = jnp.stack([spread(metric), spread(face)])

    def scratch(count):
        depth_of_work = ceil_to((segments // 2 - 1) * count, 16) + ceil_to(count, 16)
        return [
            pltpu.VMEM((segments, count, width), jnp.float32),
            pltpu.VMEM((depth_of_work, 2 * width), jnp.float32),
            pltpu.SemaphoreType.DMA,
        ]

    smooth, side = pl.pallas_call(
        filter_u_kernel,
        in_specs=[in_vmem] * 13,
        out_specs=[in_hbm, in_vmem],
        out_shape=[f32(segments, whole_block, width), f32(rows, LANES)],
        scratch_shapes=scratch(rows),
        compiler_params=params,
    )(circles_u, limit, flag, twist, weight, *matrices)
    smooth = pl.pallas_call(
        filter_v_kernel,
        in_specs=[in_vmem] * 15 + [in_hbm],
        out_specs=in_hbm,
        out_shape=f32(segments, whole_block, width),
        input_output_aliases={15: 0},
        scratch_shapes=scratch(tall),
        compiler_params=params,
    )(circles_v, limit, flag, geo, side, twist, weight, *matrices, smooth)
    winds = swap(smooth)

    step = 8
    field = pl.BlockSpec((step, rows, width), lambda i: (i, 0, 0))
    lines = lambda count: pl.BlockSpec((count, None, step, width), lambda i: (0, i, 0, 0))
    grouped = lambda x: x.reshape(x.shape[0], levels // step, step, width)
    return pl.pallas_call(
        substep_kernel,
        grid=(levels // step,),
        in_specs=[
            pl.BlockSpec((step, whole_block, width), lambda i: (i, 0, 0)),
            field,
            field,
            field,
            field,
            pl.BlockSpec((2, tall, width), lambda i: (0, 0, 0)),
            lines(5),
            lines(3),
        ],
        out_specs=[field] * 4,
        out_shape=[f32(levels, rows, width)] * 4,
        compiler_params=params,
    )(winds, adj_thick, adj_theta, theta_traj, dp_traj, geo, grouped(north), grouped(east))


def solution(mesh):
    field = P(None, "lat", "lon")
    return jax.shard_map(
        shards,
        mesh=mesh,
        in_specs=(field,) * 6 + (P(), P()),
        out_specs=(field,) * 4,
        check_vma=False,
    )
```

```python
import functools

import jax
import jax.numpy as jnp
import numpy as np
from jax import lax
from jax.experimental import pallas as pl
from jax.experimental.pallas import tpu as pltpu
from jax.sharding import PartitionSpec as P

KAPPA = 0.3
CROSS = 0.2
MERID = 0.3
LANES = 128
PAD_ROWS = 8
VMEM_LIMIT = 24 * 1024 * 1024
VMEM_LARGE = 56 * 1024 * 1024


def filter_tables(segments, width):
    length = segments * width
    half = segments // 2
    b = np.arange(width)
    angle = 2.0 * np.pi * (np.outer(b, b) % width) / width
    cos, sin = np.cos(angle), np.sin(angle)
    forward = np.block([[cos, -sin], [sin, cos]])
    n = np.arange(2 * width)
    real_angle = 2.0 * np.pi * (np.outer(n, np.arange(width + 1)) % (2 * width)) / (2 * width)
    real_forward = np.concatenate([np.cos(real_angle), -np.sin(real_angle[:, 1:width])], axis=1)
    twist = 2.0 * np.pi * np.outer(np.arange(1, half), b) / length
    twist_tables = np.stack([np.cos(twist), np.sin(twist)])
    waves = np.zeros((half, 2 * width))
    waves[0] = half * np.concatenate([np.arange(width + 1), np.arange(1, width)])
    for c in range(1, half):
        waves[c] = np.tile(c + segments * b, 2)
    folded = np.minimum(waves, length - waves)
    scale = np.where(folded < length // 2, 2.0 / length, 0.0)
    scale[0, 0] = 1.0 / length
    bound = scale / np.maximum(folded, 1.0) ** 2

    def split(matrix):
        matrix = matrix.astype(np.float32)
        high = matrix.astype(jnp.bfloat16)
        low = (matrix - high.astype(np.float32)).astype(jnp.bfloat16)
        return [jnp.asarray(high), jnp.asarray(low)]

    matrices = split(forward) + split(real_forward) + split(forward.T) + split(real_forward.T)
    return (
        matrices,
        jnp.asarray(twist_tables, jnp.float32),
        jnp.asarray(np.stack([scale, bound]), jnp.float32),
    )


def split_product(values, high_ref, low_ref):
    high = values.astype(jnp.bfloat16)
    low = (values - high.astype(jnp.float32)).astype(jnp.bfloat16)
    product = functools.partial(jnp.dot, preferred_element_type=jnp.float32)
    return (
        product(high, high_ref[...])
        + (product(low, high_ref[...]) + product(high, low_ref[...]))
    )


A1, B1, G1 = (float(np.cos(np.pi / 8)), float(np.cos(np.pi / 4)), float(np.cos(3 * np.pi / 8)))
ODD = {
    1: ((A1, B1, G1), (G1, B1, A1), 1.0),
    3: ((G1, -B1, -A1), (A1, B1, -G1), -1.0),
    5: ((-G1, -B1, A1), (A1, -B1, -G1), 1.0),
    7: ((-A1, B1, -G1), (G1, -B1, A1), -1.0),
}


def segment_transform(x):
    e = [x[j] + x[j + 8] for j in range(8)]
    o = [x[j] - x[j + 8] for j in range(8)]
    f = [e[j] + e[j + 4] for j in range(4)]
    g = [e[j] - e[j + 4] for j in range(4)]
    out = {4: (f[0] - f[2], f[3] - f[1])}
    minus, plus = B1 * (g[1] - g[3]), B1 * (g[1] + g[3])
    out[2] = (g[0] + minus, -g[2] - plus)
    out[6] = (g[0] - minus, g[2] - plus)
    d = [o[j] - o[8 - j] for j in (1, 2, 3)]
    s = [o[j] + o[8 - j] for j in (1, 2, 3)]
    for c, (cos, sin, sign) in ODD.items():
        real = o[0] + cos[0] * d[0] + cos[1] * d[1] + cos[2] * d[2]
        imag = -(sign * o[4] + sin[0] * s[0] + sin[1] * s[1] + sin[2] * s[2])
        out[c] = (real, imag)
    return (f[0] + f[2], f[1] + f[3]), out


def segment_inverse(even, odd, z):
    quarter = [z[4][0], -z[4][1], -z[4][0], z[4][1]]
    f = [(even if j % 2 == 0 else odd) + quarter[j] for j in range(4)]
    r_minus, i_minus = z[2][0] - z[6][0], z[6][1] - z[2][1]
    r_plus, i_plus = z[2][0] + z[6][0], z[2][1] + z[6][1]
    g = [r_plus, B1 * (r_minus - i_plus), i_minus, -B1 * (r_minus + i_plus)]
    e = [f[j] + g[j] for j in range(4)] + [f[j] - g[j] for j in range(4)]
    o = [None] * 8
    o[0] = z[1][0] + z[3][0] + z[5][0] + z[7][0]
    o[4] = -(z[1][1] - z[3][1] + z[5][1] - z[7][1])
    for j in (1, 2, 3):
        d = sum(ODD[c][0][j - 1] * z[c][0] for c in (1, 3, 5, 7))
        s = -sum(ODD[c][1][j - 1] * z[c][1] for c in (1, 3, 5, 7))
        o[j] = d + s
        o[8 - j] = s - d
    return [e[j] + o[j] for j in range(8)] + [e[j] - o[j] for j in range(8)]


def ceil_to(value, step):
    return -(-value // step) * step


def filter_body(x_ref, limit_ref, flag_ref, twist_ref, weight_ref, matrices, out_ref, work_ref, emit=None):
    segments, rows, width = x_ref.shape
    half = segments // 2
    base = ceil_to((half - 1) * rows, 16)
    forward, forward_low, real, real_low, back, back_low, real_back, real_back_low = matrices
    group = PAD_ROWS

    @pl.loop(0, rows // group)
    def _(step):
        at = pl.multiple_of(step * group, group)
        here = pl.ds(at, group)
        (even, odd), classes = segment_transform([x_ref[a, here, :] for a in range(segments)])
        to = pl.ds(pl.multiple_of(base + at, group), group)
        work_ref[to, :width] = even
        work_ref[to, width:] = odd
        for c in range(1, half):
            re, im = classes[c]
            cos, sin = twist_ref[0, c - 1 : c, :], twist_ref[1, c - 1 : c, :]
            to = pl.ds(pl.multiple_of((c - 1) * rows + at, group), group)
            work_ref[to, :width] = re * cos + im * sin
            work_ref[to, width:] = im * cos - re * sin

    limit = limit_ref[:rows, :]
    limit = limit * limit
    limit = jnp.concatenate([limit, limit], axis=1)

    def weights(c):
        return jnp.minimum(weight_ref[0, c : c + 1, :], limit * weight_ref[1, c : c + 1, :])

    spectrum = split_product(work_ref[:base, :], forward, forward_low)
    damping = [weights(c) for c in range(1, half)]
    if base > (half - 1) * rows:
        damping.append(jnp.zeros((base - (half - 1) * rows, 2 * width), jnp.float32))
    spectrum = spectrum * jnp.concatenate(damping, axis=0)
    work_ref[:base, :] = split_product(spectrum, back, back_low)
    spectrum = split_product(work_ref[base : base + rows, :], real, real_low) * weights(0)
    work_ref[base : base + rows, :] = split_product(spectrum, real_back, real_back_low)

    def finish(at):
        here = pl.ds(at, group)
        first = pl.ds(pl.multiple_of(base + at, group), group)
        z = {}
        for c in range(1, half):
            cos, sin = twist_ref[0, c - 1 : c, :], twist_ref[1, c - 1 : c, :]
            frm = pl.ds(pl.multiple_of((c - 1) * rows + at, group), group)
            re, im = work_ref[frm, :width], work_ref[frm, width:]
            z[c] = (re * cos - im * sin, re * sin + im * cos)
        smooth = segment_inverse(work_ref[first, :width], work_ref[first, width:], z)
        flagged = flag_ref[here, :] > 0.0
        for a in range(segments):
            out_ref[a, here, :] = jnp.where(flagged, smooth[a], x_ref[a, here, :])

    @pl.loop(0, rows // group - 1)
    def _(step):
        at = pl.multiple_of(step * group, group)
        finish(at)
        if emit:
            emit(step).start()

    finish(rows - group)


def lane_index(shape):
    return lax.broadcasted_iota(jnp.int32, shape, len(shape) - 1)


def gather_columns(out_ref, rows, picks):
    shape = (rows, LANES)
    lanes = lane_index(shape)
    total = jnp.zeros(shape, jnp.float32)
    for q, a, lane in picks:
        column = jnp.broadcast_to(out_ref[a, :rows, lane : lane + 1], shape)
        total = jnp.where(lanes == q, column, total)
    return total


def edge_kernel(u_ref, v_first_ref, v_last_ref, thick_ref, theta_ref, traj_ref, depth_ref, north_ref, south_ref):
    traj, depth = traj_ref[:, 0, :], depth_ref[:, 0, :]
    north_ref[0] = thick_ref[:, 0, :] + KAPPA * (traj / depth) * theta_ref[:, 0, :]
    north_ref[1] = traj
    north_ref[2] = depth
    north_ref[3] = u_ref[:, 0, :]
    north_ref[4] = v_first_ref[:, 0, :]
    south_ref[...] = v_last_ref[:, PAD_ROWS - 1, :]


def pair_kernel(v_ref, south_ref, north_ref, out_ref):
    rows = v_ref.shape[1]
    out_ref[:, :rows, :] = v_ref[...]
    out_ref[:, rows:, :] = jnp.zeros(out_ref[:, rows:, :].shape, jnp.float32)
    out_ref[:, rows, :] = south_ref[...]
    out_ref[:, rows + 1, :] = north_ref[4]
    out_ref[:, rows + 2, :] = north_ref[3]


def rows_kernel(limits_ref, flags_ref, limit_block_ref, flag_block_ref, limit_out, flag_out, line_ref):
    rows = limit_out.shape[0] - PAD_ROWS
    count = limits_ref.shape[0]
    first = lax.axis_index("lat") * rows
    south, north = jnp.maximum(first - 1, 0), jnp.minimum(first + rows, count - 1)
    sub = lax.broadcasted_iota(jnp.int32, (PAD_ROWS, LANES), 0)
    for block_ref, scalar_ref, out_ref in (
        (limit_block_ref, limits_ref, limit_out),
        (flag_block_ref, flags_ref, flag_out),
    ):
        line = block_ref[pl.ds(first // LANES, 1), :].astype(jnp.float32)
        line_ref[...] = jnp.broadcast_to(line, (LANES, LANES)).T
        out_ref[:rows, :] = line_ref[pl.ds(pl.multiple_of(first % LANES, rows), rows), :]
        tail = jnp.where(sub == 0, scalar_ref[south], scalar_ref[north])
        out_ref[rows:, :] = tail.astype(jnp.float32)


def filter_u_kernel(x_ref, limit_ref, flag_ref, twist_ref, weight_ref, *rest):
    matrices, (out_ref, side_ref, smooth_ref, work_ref, sem) = rest[:8], rest[8:]
    segments, rows, width = x_ref.shape
    filter_body(x_ref, limit_ref, flag_ref, twist_ref, weight_ref, matrices, smooth_ref, work_ref)
    copy = pltpu.make_async_copy(smooth_ref, out_ref.at[:, :rows, :], sem)
    copy.start()
    last = width - 1
    ahead = [(a, (a + 1) % segments, 0) for a in range(segments)]
    behind = [(segments + a, (a - 1) % segments, last) for a in range(segments)]
    own = [(a, a, last) for a in range(segments)]
    side_ref[...] = gather_columns(smooth_ref, rows, ahead + behind) - gather_columns(smooth_ref, rows, own)
    copy.wait()


def filter_v_kernel(x_ref, limit_ref, flag_ref, geo_ref, side_ref, twist_ref, weight_ref, *rest):
    matrices, (_, out_ref, smooth_ref, work_ref, sem) = rest[:8], rest[8:]
    segments, tall, width = x_ref.shape
    rows = tall - PAD_ROWS

    def emit(step):
        at = pl.multiple_of(step * PAD_ROWS, PAD_ROWS)
        source = smooth_ref.at[:, pl.ds(at, PAD_ROWS), :]
        return pltpu.make_async_copy(source, out_ref.at[:, pl.ds(rows + at, PAD_ROWS), :], sem.at[step])

    filter_body(x_ref, limit_ref, flag_ref, twist_ref, weight_ref, matrices, smooth_ref, work_ref, emit)
    metric = geo_ref[0, :rows, :]
    metric_north = geo_ref[0, rows : rows + 1, :]
    edge = lane_index((1, width)) == 0
    u_north = [smooth_ref[a, rows + 2 : rows + 3, :] for a in range(segments)]
    rolled = [pltpu.roll(u_north[a], 1, 1) for a in range(segments)]
    ahead = [(a, (a + 1) % segments, 0) for a in range(segments)]
    v_ahead = gather_columns(smooth_ref, rows + 1, ahead)
    v_body = v_ahead[:rows]
    top = lax.broadcasted_iota(jnp.int32, (rows, LANES), 0) == 0
    v_south = jnp.where(top, v_ahead[rows : rows + 1], pltpu.roll(v_body, 1, 0))
    side = side_ref[...]
    mixed = CROSS * metric * side + MERID * (v_body - v_south)
    columns = jnp.where(lane_index((rows, LANES)) < segments, mixed, side)
    columns = jnp.concatenate([columns, jnp.zeros((LANES - rows, LANES), jnp.float32)], axis=0).T
    for a in range(segments):
        west = jnp.where(edge, rolled[a - 1], rolled[a])
        smooth_ref[a, rows + 1 : rows + 2, :] = CROSS * metric_north * (u_north[a] - west) + MERID * (
            smooth_ref[a, rows + 1 : rows + 2, :] - smooth_ref[a, rows - 1 : rows, :]
        )
        smooth_ref[a, rows + 2 : rows + 3, :] = columns[a : a + 1]
        smooth_ref[a, rows + 3 : rows + 4, :] = columns[segments + a : segments + a + 1]
    emit(rows // PAD_ROWS).start()

    @pl.loop(0, tall // PAD_ROWS)
    def _(step):
        emit(step).wait()


def substep_kernel(
    winds_ref, thick_ref, theta_ref, traj_ref, depth_ref, geo_ref, north_ref, east_ref,
    u_out, v_out, theta_out, thick_out,
):
    levels, rows, width = thick_ref.shape
    main = 2 * rows
    metric, face = geo_ref[0, :rows, :], geo_ref[1, :rows, :]
    metric_north = geo_ref[0, rows : rows + 1, :]
    shape = (rows, width)
    lanes, sub = lane_index(shape), lax.broadcasted_iota(jnp.int32, shape, 0)
    first_lane, last_lane = lanes == 0, lanes == width - 1
    first_row, last_row = sub == 0, sub == rows - 1
    lines = []
    for k in range(levels):
        ga_east = winds_ref[k, main + 2 : main + 3, :]
        lines.append(east_ref[0, k : k + 1, :] + (1.0 + KAPPA) * east_ref[1, k : k + 1, :] * ga_east)
    for k in range(levels):
        lines.append(east_ref[2, k : k + 1, :])
    for k in range(levels):
        lines.append(winds_ref[k, main + 3 : main + 4, :])
    lines.append(jnp.zeros((LANES - 3 * levels, width), jnp.float32))
    columns = jnp.concatenate(lines, axis=0).T
    for k in range(levels):
        ua, va = winds_ref[k, :rows, :], winds_ref[k, rows:main, :]
        traj, depth = traj_ref[k], depth_ref[k]
        e_east = jnp.broadcast_to(columns[:rows, k : k + 1], shape)
        depth_east = jnp.broadcast_to(columns[:rows, levels + k : levels + k + 1], shape)
        u_west = jnp.broadcast_to(columns[:rows, 2 * levels + k : 2 * levels + k + 1], shape)
        west = jnp.where(first_lane, u_west, pltpu.roll(ua, 1, 1))
        south = jnp.where(first_row, winds_ref[k, main : main + 1, :], pltpu.roll(va, 1, 0))
        ga = CROSS * metric * (ua - west) + MERID * (va - south)
        thick = thick_ref[k] + traj * ga
        theta = theta_ref[k] + depth * ga
        e = thick + KAPPA * (traj / depth) * theta
        e_shift = jnp.where(last_lane, e_east, pltpu.roll(e, width - 1, 1))
        depth_shift = jnp.where(last_lane, depth_east, pltpu.roll(depth, width - 1, 1))
        u_out[k] = ua + (0.5 * CROSS) * (depth + depth_shift) * metric * (e_shift - e)
        e_north = north_ref[0, k : k + 1, :] + (1.0 + KAPPA) * north_ref[1, k : k + 1, :] * winds_ref[k, main + 1 : main + 2, :]
        me = metric * e
        me_shift = jnp.where(last_row, metric_north * e_north, pltpu.roll(me, rows - 1, 0))
        depth_up = jnp.where(last_row, north_ref[2, k : k + 1, :], pltpu.roll(depth, rows - 1, 0))
        v_out[k] = va + (0.5 * MERID) * (depth + depth_up) * face * (me_shift - me)
        theta_out[k] = theta
        thick_out[k] = thick


def row_geometry(row_index, total_rows):
    position = row_index.astype(jnp.float32)
    centre = jnp.pi * ((position + 0.5) / total_rows - 0.5)
    face = jnp.pi * ((position + 1.0) / total_rows - 0.5)
    return (jnp.cos(face), 1.0 / (jnp.cos(centre) + 0.25))


def spread(column):
    return jnp.broadcast_to(column[:, None], (column.shape[0], LANES))


def swap(blocks):
    return lax.all_to_all(blocks, "lon", split_axis=0, concat_axis=0, tiled=True)


def shards(adj_u, adj_v, adj_theta, adj_thick, theta_traj, dp_traj, cutoff, polar_flags):
    levels, rows, width = adj_u.shape
    bands, segments = lax.axis_size("lat"), lax.axis_size("lon")
    band = lax.axis_index("lat")
    total_rows = rows * bands
    tall, whole_block = rows + PAD_ROWS, 2 * rows + PAD_ROWS
    matrices, twist, weight = filter_tables(segments, width)
    params = pltpu.CompilerParams(vmem_limit_bytes=VMEM_LIMIT)
    large = pltpu.CompilerParams(vmem_limit_bytes=VMEM_LARGE)
    in_vmem = pl.BlockSpec(memory_space=pltpu.VMEM)
    in_hbm = pl.BlockSpec(memory_space=pltpu.HBM)
    in_smem = pl.BlockSpec(memory_space=pltpu.SMEM)
    hbm = lambda *shape: pltpu.HBM(shape, jnp.float32)
    f32 = lambda *shape: jax.ShapeDtypeStruct(shape, jnp.float32)
    north_to_south = [(i + 1, i) for i in range(bands - 1)]
    south_to_north = [(i, i + 1) for i in range(bands - 1)]
    east_to_west = [((i + 1) % segments, i) for i in range(segments)]

    circles_u = swap(adj_u)

    block = lambda at: pl.BlockSpec((levels, PAD_ROWS, width), lambda i, at=at: (0, at, 0))
    first, last = block(0), block(rows // PAD_ROWS - 1)
    to_south, to_north = pl.pallas_call(
        edge_kernel,
        grid=(1,),
        in_specs=[first, first, last, first, first, first, first],
        out_specs=[
            pl.BlockSpec((5, levels, width), lambda i: (0, 0, 0)),
            pl.BlockSpec((levels, width), lambda i: (0, 0)),
        ],
        out_shape=[f32(5, levels, width), f32(levels, width)],
        compiler_params=large,
    )(adj_u, adj_v, adj_v, adj_thick, adj_theta, theta_traj, dp_traj)
    north = lax.ppermute(to_south, "lat", north_to_south)
    south = lax.ppermute(to_north, "lat", south_to_north)
    step = 8
    circles_v = swap(
        pl.pallas_call(
            pair_kernel,
            grid=(levels // step,),
            in_specs=[
                pl.BlockSpec((step, rows, width), lambda i: (i, 0, 0)),
                pl.BlockSpec((step, width), lambda i: (i, 0)),
                pl.BlockSpec((5, step, width), lambda i: (0, i, 0)),
            ],
            out_specs=pl.BlockSpec((step, tall, width), lambda i: (i, 0, 0)),
            out_shape=hbm(levels, tall, width),
            compiler_params=params,
        )(adj_v, south, north)
    )

    first_column = lambda x: x[:, :, 0]
    traj, depth = first_column(theta_traj), first_column(dp_traj)
    change = first_column(adj_thick) + KAPPA * (traj / depth) * first_column(adj_theta)
    east = jnp.stack([change, traj, depth])
    east = jnp.pad(east, ((0, 0), (0, 0), (0, LANES - rows)))
    east = lax.ppermute(east, "lon", east_to_west)

    limit, flag = pl.pallas_call(
        rows_kernel,
        in_specs=[in_smem, in_smem, in_vmem, in_vmem],
        out_specs=[in_vmem] * 2,
        out_shape=[f32(tall, LANES)] * 2,
        scratch_shapes=[pltpu.VMEM((LANES, LANES), jnp.float32)],
        compiler_params=params,
    )(cutoff, polar_flags, cutoff.reshape(-1, LANES), polar_flags.reshape(-1, LANES))
    face, metric = row_geometry(band * rows + jnp.arange(tall, dtype=jnp.int32), total_rows)
    geo = jnp.stack([spread(metric), spread(face)])

    def scratch(count, copies):
        depth_of_work = ceil_to((segments // 2 - 1) * count, 16) + ceil_to(count, 16)
        return [
            pltpu.VMEM((segments, count, width), jnp.float32),
            pltpu.VMEM((depth_of_work, 2 * width), jnp.float32),
            copies,
        ]

    smooth, side = pl.pallas_call(
        filter_u_kernel,
        in_specs=[in_vmem] * 13,
        out_specs=[in_hbm, in_vmem],
        out_shape=[hbm(segments, whole_block, width), f32(rows, LANES)],
        scratch_shapes=scratch(rows, pltpu.SemaphoreType.DMA),
        compiler_params=params,
    )(circles_u, limit, flag, twist, weight, *matrices)
    smooth = pl.pallas_call(
        filter_v_kernel,
        in_specs=[in_vmem] * 15 + [in_hbm],
        out_specs=in_hbm,
        out_shape=hbm(segments, whole_block, width),
        input_output_aliases={15: 0},
        scratch_shapes=scratch(tall, pltpu.SemaphoreType.DMA((tall // PAD_ROWS,))),
        compiler_params=params,
    )(circles_v, limit, flag, geo, side, twist, weight, *matrices, smooth)
    winds = swap(smooth)

    step = 8
    field = pl.BlockSpec((step, rows, width), lambda i: (i, 0, 0))
    lines = lambda count: pl.BlockSpec((count, None, step, width), lambda i: (0, i, 0, 0))
    grouped = lambda x: x.reshape(x.shape[0], levels // step, step, width)
    return pl.pallas_call(
        substep_kernel,
        grid=(levels // step,),
        in_specs=[
            pl.BlockSpec((step, whole_block, width), lambda i: (i, 0, 0)),
            field,
            field,
            field,
            field,
            pl.BlockSpec((2, tall, width), lambda i: (0, 0, 0)),
            lines(5),
            lines(3),
        ],
        out_specs=[field] * 4,
        out_shape=[f32(levels, rows, width)] * 4,
        compiler_params=params,
    )(winds, adj_thick, adj_theta, theta_traj, dp_traj, geo, grouped(north), grouped(east))


def solution(mesh):
    field = P(None, "lat", "lon")
    return jax.shard_map(
        shards,
        mesh=mesh,
        in_specs=(field,) * 6 + (P(), P()),
        out_specs=(field,) * 4,
        check_vma=False,
    )
```

```python
import functools

import jax
import jax.numpy as jnp
import numpy as np
from jax import lax
from jax.experimental import pallas as pl
from jax.experimental.pallas import tpu as pltpu
from jax.sharding import PartitionSpec as P

KAPPA = 0.3
CROSS = 0.2
MERID = 0.3
LANES = 128
PAD_ROWS = 8
VMEM_LIMIT = 24 * 1024 * 1024
VMEM_LARGE = 56 * 1024 * 1024


def filter_tables(segments, width):
    length = segments * width
    half = segments // 2
    b = np.arange(width)
    angle = 2.0 * np.pi * (np.outer(b, b) % width) / width
    cos, sin = np.cos(angle), np.sin(angle)
    forward = np.block([[cos, -sin], [sin, cos]])
    n = np.arange(2 * width)
    real_angle = 2.0 * np.pi * (np.outer(n, np.arange(width + 1)) % (2 * width)) / (2 * width)
    real_forward = np.concatenate([np.cos(real_angle), -np.sin(real_angle[:, 1:width])], axis=1)
    twist = 2.0 * np.pi * np.outer(np.arange(1, half), b) / length
    twist_tables = np.stack([np.cos(twist), np.sin(twist)])
    waves = np.zeros((half, 2 * width))
    waves[0] = half * np.concatenate([np.arange(width + 1), np.arange(1, width)])
    for c in range(1, half):
        waves[c] = np.tile(c + segments * b, 2)
    folded = np.minimum(waves, length - waves)
    scale = np.where(folded < length // 2, 2.0 / length, 0.0)
    scale[0, 0] = 1.0 / length
    bound = scale / np.maximum(folded, 1.0) ** 2

    def split(matrix):
        matrix = matrix.astype(np.float32)
        high = matrix.astype(jnp.bfloat16)
        low = (matrix - high.astype(np.float32)).astype(jnp.bfloat16)
        return [jnp.asarray(np.concatenate([high, high, low]))]

    matrices = split(forward) + split(real_forward) + split(forward.T) + split(real_forward.T)
    return (
        matrices,
        jnp.asarray(twist_tables, jnp.float32),
        jnp.asarray(np.stack([scale, bound]), jnp.float32),
    )


def split_product(values, stacked_ref):
    high = values.astype(jnp.bfloat16)
    low = (values - high.astype(jnp.float32)).astype(jnp.bfloat16)
    parts = jnp.concatenate([high, low, high], axis=1)
    return jnp.dot(parts, stacked_ref[...], preferred_element_type=jnp.float32)


A1, B1, G1 = (float(np.cos(np.pi / 8)), float(np.cos(np.pi / 4)), float(np.cos(3 * np.pi / 8)))
ODD = {
    1: ((A1, B1, G1), (G1, B1, A1), 1.0),
    3: ((G1, -B1, -A1), (A1, B1, -G1), -1.0),
    5: ((-G1, -B1, A1), (A1, -B1, -G1), 1.0),
    7: ((-A1, B1, -G1), (G1, -B1, A1), -1.0),
}


def segment_transform(x):
    e = [x[j] + x[j + 8] for j in range(8)]
    o = [x[j] - x[j + 8] for j in range(8)]
    f = [e[j] + e[j + 4] for j in range(4)]
    g = [e[j] - e[j + 4] for j in range(4)]
    out = {4: (f[0] - f[2], f[3] - f[1])}
    minus, plus = B1 * (g[1] - g[3]), B1 * (g[1] + g[3])
    out[2] = (g[0] + minus, -g[2] - plus)
    out[6] = (g[0] - minus, g[2] - plus)
    d = [o[j] - o[8 - j] for j in (1, 2, 3)]
    s = [o[j] + o[8 - j] for j in (1, 2, 3)]
    for c, (cos, sin, sign) in ODD.items():
        real = o[0] + cos[0] * d[0] + cos[1] * d[1] + cos[2] * d[2]
        imag = -(sign * o[4] + sin[0] * s[0] + sin[1] * s[1] + sin[2] * s[2])
        out[c] = (real, imag)
    return (f[0] + f[2], f[1] + f[3]), out


def segment_inverse(even, odd, z):
    quarter = [z[4][0], -z[4][1], -z[4][0], z[4][1]]
    f = [(even if j % 2 == 0 else odd) + quarter[j] for j in range(4)]
    r_minus, i_minus = z[2][0] - z[6][0], z[6][1] - z[2][1]
    r_plus, i_plus = z[2][0] + z[6][0], z[2][1] + z[6][1]
    g = [r_plus, B1 * (r_minus - i_plus), i_minus, -B1 * (r_minus + i_plus)]
    e = [f[j] + g[j] for j in range(4)] + [f[j] - g[j] for j in range(4)]
    o = [None] * 8
    o[0] = z[1][0] + z[3][0] + z[5][0] + z[7][0]
    o[4] = -(z[1][1] - z[3][1] + z[5][1] - z[7][1])
    for j in (1, 2, 3):
        d = sum(ODD[c][0][j - 1] * z[c][0] for c in (1, 3, 5, 7))
        s = -sum(ODD[c][1][j - 1] * z[c][1] for c in (1, 3, 5, 7))
        o[j] = d + s
        o[8 - j] = s - d
    return [e[j] + o[j] for j in range(8)] + [e[j] - o[j] for j in range(8)]


def ceil_to(value, step):
    return -(-value // step) * step


def filter_body(x_ref, limit_ref, flag_ref, twist_ref, weight_ref, matrices, out_ref, work_ref, emit=None):
    segments, rows, width = x_ref.shape
    half = segments // 2
    base = ceil_to((half - 1) * rows, 16)
    forward, real, back, real_back = matrices
    group = PAD_ROWS

    @pl.loop(0, rows // group)
    def _(step):
        at = pl.multiple_of(step * group, group)
        here = pl.ds(at, group)
        (even, odd), classes = segment_transform([x_ref[a, here, :] for a in range(segments)])
        to = pl.ds(pl.multiple_of(base + at, group), group)
        work_ref[to, :width] = even
        work_ref[to, width:] = odd
        for c in range(1, half):
            re, im = classes[c]
            cos, sin = twist_ref[0, c - 1 : c, :], twist_ref[1, c - 1 : c, :]
            to = pl.ds(pl.multiple_of((c - 1) * rows + at, group), group)
            work_ref[to, :width] = re * cos + im * sin
            work_ref[to, width:] = im * cos - re * sin

    limit = limit_ref[:rows, :]
    limit = limit * limit
    limit = jnp.concatenate([limit, limit], axis=1)

    def weights(c):
        return jnp.minimum(weight_ref[0, c : c + 1, :], limit * weight_ref[1, c : c + 1, :])

    spectrum = split_product(work_ref[:base, :], forward)
    damping = [weights(c) for c in range(1, half)]
    if base > (half - 1) * rows:
        damping.append(jnp.zeros((base - (half - 1) * rows, 2 * width), jnp.float32))
    spectrum = spectrum * jnp.concatenate(damping, axis=0)
    work_ref[:base, :] = split_product(spectrum, back)
    spectrum = split_product(work_ref[base : base + rows, :], real) * weights(0)
    work_ref[base : base + rows, :] = split_product(spectrum, real_back)

    def finish(at):
        here = pl.ds(at, group)
        first = pl.ds(pl.multiple_of(base + at, group), group)
        z = {}
        for c in range(1, half):
            cos, sin = twist_ref[0, c - 1 : c, :], twist_ref[1, c - 1 : c, :]
            frm = pl.ds(pl.multiple_of((c - 1) * rows + at, group), group)
            re, im = work_ref[frm, :width], work_ref[frm, width:]
            z[c] = (re * cos - im * sin, re * sin + im * cos)
        smooth = segment_inverse(work_ref[first, :width], work_ref[first, width:], z)
        flagged = flag_ref[here, :] > 0.0
        for a in range(segments):
            out_ref[a, here, :] = jnp.where(flagged, smooth[a], x_ref[a, here, :])

    @pl.loop(0, rows // group - 1)
    def _(step):
        at = pl.multiple_of(step * group, group)
        finish(at)
        if emit:
            emit(step).start()

    finish(rows - group)


def lane_index(shape):
    return lax.broadcasted_iota(jnp.int32, shape, len(shape) - 1)


def gather_columns(out_ref, rows, picks):
    shape = (rows, LANES)
    lanes = lane_index(shape)
    total = jnp.zeros(shape, jnp.float32)
    for q, a, lane in picks:
        column = jnp.broadcast_to(out_ref[a, :rows, lane : lane + 1], shape)
        total = jnp.where(lanes == q, column, total)
    return total


def edge_kernel(u_ref, v_first_ref, v_last_ref, thick_ref, theta_ref, traj_ref, depth_ref, north_ref, south_ref):
    traj, depth = traj_ref[:, 0, :], depth_ref[:, 0, :]
    north_ref[0] = thick_ref[:, 0, :] + KAPPA * (traj / depth) * theta_ref[:, 0, :]
    north_ref[1] = traj
    north_ref[2] = depth
    north_ref[3] = u_ref[:, 0, :]
    north_ref[4] = v_first_ref[:, 0, :]
    south_ref[...] = v_last_ref[:, PAD_ROWS - 1, :]


def pair_kernel(v_ref, south_ref, north_ref, out_ref):
    rows = v_ref.shape[1]
    out_ref[:, :rows, :] = v_ref[...]
    out_ref[:, rows:, :] = jnp.zeros(out_ref[:, rows:, :].shape, jnp.float32)
    out_ref[:, rows, :] = south_ref[...]
    out_ref[:, rows + 1, :] = north_ref[4]
    out_ref[:, rows + 2, :] = north_ref[3]


def rows_kernel(limits_ref, flags_ref, limit_block_ref, flag_block_ref, limit_out, flag_out, line_ref):
    rows = limit_out.shape[0] - PAD_ROWS
    count = limits_ref.shape[0]
    first = lax.axis_index("lat") * rows
    south, north = jnp.maximum(first - 1, 0), jnp.minimum(first + rows, count - 1)
    sub = lax.broadcasted_iota(jnp.int32, (PAD_ROWS, LANES), 0)
    for block_ref, scalar_ref, out_ref in (
        (limit_block_ref, limits_ref, limit_out),
        (flag_block_ref, flags_ref, flag_out),
    ):
        line = block_ref[pl.ds(first // LANES, 1), :].astype(jnp.float32)
        line_ref[...] = jnp.broadcast_to(line, (LANES, LANES)).T
        out_ref[:rows, :] = line_ref[pl.ds(pl.multiple_of(first % LANES, rows), rows), :]
        tail = jnp.where(sub == 0, scalar_ref[south], scalar_ref[north])
        out_ref[rows:, :] = tail.astype(jnp.float32)


def filter_u_kernel(x_ref, limit_ref, flag_ref, twist_ref, weight_ref, *rest):
    matrices, (out_ref, side_ref, smooth_ref, work_ref, sem) = rest[:4], rest[4:]
    segments, rows, width = x_ref.shape
    filter_body(x_ref, limit_ref, flag_ref, twist_ref, weight_ref, matrices, smooth_ref, work_ref)
    copy = pltpu.make_async_copy(smooth_ref, out_ref.at[:, :rows, :], sem)
    copy.start()
    last = width - 1
    ahead = [(a, (a + 1) % segments, 0) for a in range(segments)]
    behind = [(segments + a, (a - 1) % segments, last) for a in range(segments)]
    own = [(a, a, last) for a in range(segments)]
    side_ref[...] = gather_columns(smooth_ref, rows, ahead + behind) - gather_columns(smooth_ref, rows, own)
    copy.wait()


def filter_v_kernel(x_ref, limit_ref, flag_ref, geo_ref, side_ref, twist_ref, weight_ref, *rest):
    matrices, (_, out_ref, smooth_ref, work_ref, sem) = rest[:4], rest[4:]
    segments, tall, width = x_ref.shape
    rows = tall - PAD_ROWS

    def emit(step):
        at = pl.multiple_of(step * PAD_ROWS, PAD_ROWS)
        source = smooth_ref.at[:, pl.ds(at, PAD_ROWS), :]
        return pltpu.make_async_copy(source, out_ref.at[:, pl.ds(rows + at, PAD_ROWS), :], sem.at[step])

    filter_body(x_ref, limit_ref, flag_ref, twist_ref, weight_ref, matrices, smooth_ref, work_ref, emit)
    metric = geo_ref[0, :rows, :]
    metric_north = geo_ref[0, rows : rows + 1, :]
    edge = lane_index((1, width)) == 0
    u_north = [smooth_ref[a, rows + 2 : rows + 3, :] for a in range(segments)]
    rolled = [pltpu.roll(u_north[a], 1, 1) for a in range(segments)]
    ahead = [(a, (a + 1) % segments, 0) for a in range(segments)]
    v_ahead = gather_columns(smooth_ref, rows + 1, ahead)
    v_body = v_ahead[:rows]
    top = lax.broadcasted_iota(jnp.int32, (rows, LANES), 0) == 0
    v_south = jnp.where(top, v_ahead[rows : rows + 1], pltpu.roll(v_body, 1, 0))
    side = side_ref[...]
    mixed = CROSS * metric * side + MERID * (v_body - v_south)
    columns = jnp.where(lane_index((rows, LANES)) < segments, mixed, side)
    columns = jnp.concatenate([columns, jnp.zeros((LANES - rows, LANES), jnp.float32)], axis=0).T
    for a in range(segments):
        west = jnp.where(edge, rolled[a - 1], rolled[a])
        smooth_ref[a, rows + 1 : rows + 2, :] = CROSS * metric_north * (u_north[a] - west) + MERID * (
            smooth_ref[a, rows + 1 : rows + 2, :] - smooth_ref[a, rows - 1 : rows, :]
        )
        smooth_ref[a, rows + 2 : rows + 3, :] = columns[a : a + 1]
        smooth_ref[a, rows + 3 : rows + 4, :] = columns[segments + a : segments + a + 1]
    emit(rows // PAD_ROWS).start()

    @pl.loop(0, tall // PAD_ROWS)
    def _(step):
        emit(step).wait()


def substep_kernel(
    winds_ref, thick_ref, theta_ref, traj_ref, depth_ref, geo_ref, north_ref, east_ref,
    u_out, v_out, theta_out, thick_out,
):
    levels, rows, width = thick_ref.shape
    main = 2 * rows
    metric, face = geo_ref[0, :rows, :], geo_ref[1, :rows, :]
    metric_north = geo_ref[0, rows : rows + 1, :]
    shape = (rows, width)
    lanes, sub = lane_index(shape), lax.broadcasted_iota(jnp.int32, shape, 0)
    first_lane, last_lane = lanes == 0, lanes == width - 1
    first_row, last_row = sub == 0, sub == rows - 1
    lines = []
    for k in range(levels):
        ga_east = winds_ref[k, main + 2 : main + 3, :]
        lines.append(east_ref[0, k : k + 1, :] + (1.0 + KAPPA) * east_ref[1, k : k + 1, :] * ga_east)
    for k in range(levels):
        lines.append(east_ref[2, k : k + 1, :])
    for k in range(levels):
        lines.append(winds_ref[k, main + 3 : main + 4, :])
    lines.append(jnp.zeros((LANES - 3 * levels, width), jnp.float32))
    columns = jnp.concatenate(lines, axis=0).T
    for k in range(levels):
        ua, va = winds_ref[k, :rows, :], winds_ref[k, rows:main, :]
        traj, depth = traj_ref[k], depth_ref[k]
        e_east = jnp.broadcast_to(columns[:rows, k : k + 1], shape)
        depth_east = jnp.broadcast_to(columns[:rows, levels + k : levels + k + 1], shape)
        u_west = jnp.broadcast_to(columns[:rows, 2 * levels + k : 2 * levels + k + 1], shape)
        west = jnp.where(first_lane, u_west, pltpu.roll(ua, 1, 1))
        south = jnp.where(first_row, winds_ref[k, main : main + 1, :], pltpu.roll(va, 1, 0))
        ga = CROSS * metric * (ua - west) + MERID * (va - south)
        thick = thick_ref[k] + traj * ga
        theta = theta_ref[k] + depth * ga
        e = thick + KAPPA * (traj / depth) * theta
        e_shift = jnp.where(last_lane, e_east, pltpu.roll(e, width - 1, 1))
        depth_shift = jnp.where(last_lane, depth_east, pltpu.roll(depth, width - 1, 1))
        u_out[k] = ua + (0.5 * CROSS) * (depth + depth_shift) * metric * (e_shift - e)
        e_north = north_ref[0, k : k + 1, :] + (1.0 + KAPPA) * north_ref[1, k : k + 1, :] * winds_ref[k, main + 1 : main + 2, :]
        me = metric * e
        me_shift = jnp.where(last_row, metric_north * e_north, pltpu.roll(me, rows - 1, 0))
        depth_up = jnp.where(last_row, north_ref[2, k : k + 1, :], pltpu.roll(depth, rows - 1, 0))
        v_out[k] = va + (0.5 * MERID) * (depth + depth_up) * face * (me_shift - me)
        theta_out[k] = theta
        thick_out[k] = thick


def row_geometry(row_index, total_rows):
    position = row_index.astype(jnp.float32)
    centre = jnp.pi * ((position + 0.5) / total_rows - 0.5)
    face = jnp.pi * ((position + 1.0) / total_rows - 0.5)
    return (jnp.cos(face), 1.0 / (jnp.cos(centre) + 0.25))


def spread(column):
    return jnp.broadcast_to(column[:, None], (column.shape[0], LANES))


def swap(blocks):
    return lax.all_to_all(blocks, "lon", split_axis=0, concat_axis=0, tiled=True)


def shards(adj_u, adj_v, adj_theta, adj_thick, theta_traj, dp_traj, cutoff, polar_flags):
    levels, rows, width = adj_u.shape
    bands, segments = lax.axis_size("lat"), lax.axis_size("lon")
    band = lax.axis_index("lat")
    total_rows = rows * bands
    tall, whole_block = rows + PAD_ROWS, 2 * rows + PAD_ROWS
    matrices, twist, weight = filter_tables(segments, width)
    params = pltpu.CompilerParams(vmem_limit_bytes=VMEM_LIMIT)
    large = pltpu.CompilerParams(vmem_limit_bytes=VMEM_LARGE)
    in_vmem = pl.BlockSpec(memory_space=pltpu.VMEM)
    in_hbm = pl.BlockSpec(memory_space=pltpu.HBM)
    in_smem = pl.BlockSpec(memory_space=pltpu.SMEM)
    hbm = lambda *shape: pltpu.HBM(shape, jnp.float32)
    f32 = lambda *shape: jax.ShapeDtypeStruct(shape, jnp.float32)
    north_to_south = [(i + 1, i) for i in range(bands - 1)]
    south_to_north = [(i, i + 1) for i in range(bands - 1)]
    east_to_west = [((i + 1) % segments, i) for i in range(segments)]

    circles_u = swap(adj_u)

    block = lambda at: pl.BlockSpec((levels, PAD_ROWS, width), lambda i, at=at: (0, at, 0))
    first, last = block(0), block(rows // PAD_ROWS - 1)
    to_south, to_north = pl.pallas_call(
        edge_kernel,
        grid=(1,),
        in_specs=[first, first, last, first, first, first, first],
        out_specs=[
            pl.BlockSpec((5, levels, width), lambda i: (0, 0, 0)),
            pl.BlockSpec((levels, width), lambda i: (0, 0)),
        ],
        out_shape=[f32(5, levels, width), f32(levels, width)],
        compiler_params=large,
    )(adj_u, adj_v, adj_v, adj_thick, adj_theta, theta_traj, dp_traj)
    north = lax.ppermute(to_south, "lat", north_to_south)
    south = lax.ppermute(to_north, "lat", south_to_north)
    step = 8
    circles_v = swap(
        pl.pallas_call(
            pair_kernel,
            grid=(levels // step,),
            in_specs=[
                pl.BlockSpec((step, rows, width), lambda i: (i, 0, 0)),
                pl.BlockSpec((step, width), lambda i: (i, 0)),
                pl.BlockSpec((5, step, width), lambda i: (0, i, 0)),
            ],
            out_specs=pl.BlockSpec((step, tall, width), lambda i: (i, 0, 0)),
            out_shape=hbm(levels, tall, width),
            compiler_params=params,
        )(adj_v, south, north)
    )

    first_column = lambda x: x[:, :, 0]
    traj, depth = first_column(theta_traj), first_column(dp_traj)
    change = first_column(adj_thick) + KAPPA * (traj / depth) * first_column(adj_theta)
    east = jnp.stack([change, traj, depth])
    east = jnp.pad(east, ((0, 0), (0, 0), (0, LANES - rows)))
    east = lax.ppermute(east, "lon", east_to_west)

    limit, flag = pl.pallas_call(
        rows_kernel,
        in_specs=[in_smem, in_smem, in_vmem, in_vmem],
        out_specs=[in_vmem] * 2,
        out_shape=[f32(tall, LANES)] * 2,
        scratch_shapes=[pltpu.VMEM((LANES, LANES), jnp.float32)],
        compiler_params=params,
    )(cutoff, polar_flags, cutoff.reshape(-1, LANES), polar_flags.reshape(-1, LANES))
    face, metric = row_geometry(band * rows + jnp.arange(tall, dtype=jnp.int32), total_rows)
    geo = jnp.stack([spread(metric), spread(face)])

    def scratch(count, copies):
        depth_of_work = ceil_to((segments // 2 - 1) * count, 16) + ceil_to(count, 16)
        return [
            pltpu.VMEM((segments, count, width), jnp.float32),
            pltpu.VMEM((depth_of_work, 2 * width), jnp.float32),
            copies,
        ]

    smooth, side = pl.pallas_call(
        filter_u_kernel,
        in_specs=[in_vmem] * 9,
        out_specs=[in_hbm, in_vmem],
        out_shape=[hbm(segments, whole_block, width), f32(rows, LANES)],
        scratch_shapes=scratch(rows, pltpu.SemaphoreType.DMA),
        compiler_params=params,
    )(circles_u, limit, flag, twist, weight, *matrices)
    smooth = pl.pallas_call(
        filter_v_kernel,
        in_specs=[in_vmem] * 11 + [in_hbm],
        out_specs=in_hbm,
        out_shape=hbm(segments, whole_block, width),
        input_output_aliases={11: 0},
        scratch_shapes=scratch(tall, pltpu.SemaphoreType.DMA((tall // PAD_ROWS,))),
        compiler_params=params,
    )(circles_v, limit, flag, geo, side, twist, weight, *matrices, smooth)
    winds = swap(smooth)

    step = 8
    field = pl.BlockSpec((step, rows, width), lambda i: (i, 0, 0))
    lines = lambda count: pl.BlockSpec((count, None, step, width), lambda i: (0, i, 0, 0))
    grouped = lambda x: x.reshape(x.shape[0], levels // step, step, width)
    return pl.pallas_call(
        substep_kernel,
        grid=(levels // step,),
        in_specs=[
            pl.BlockSpec((step, whole_block, width), lambda i: (i, 0, 0)),
            field,
            field,
            field,
            field,
            pl.BlockSpec((2, tall, width), lambda i: (0, 0, 0)),
            lines(5),
            lines(3),
        ],
        out_specs=[field] * 4,
        out_shape=[f32(levels, rows, width)] * 4,
        compiler_params=params,
    )(winds, adj_thick, adj_theta, theta_traj, dp_traj, geo, grouped(north), grouped(east))


def solution(mesh):
    field = P(None, "lat", "lon")
    return jax.shard_map(
        shards,
        mesh=mesh,
        in_specs=(field,) * 6 + (P(), P()),
        out_specs=(field,) * 4,
        check_vma=False,
    )
```
